32 devices in a mesh: modes: 16 (over z, y, x), grp: 2 (over core).
Axes of the slice: x: 2, y: 2, z: 4, core: 2. Of those that a mesh axis runs over, the one named last changes fastest.
Arguments:
- left_core: bfloat16 [32768, 512], P(('modes', 'grp')), may hold values from -6 to 6
- right_core: bfloat16 [32768, 512], P(('modes', 'grp')), may hold values from -6 to 6
- gauss_core: bfloat16 [32768, 256], P(('modes', 'grp')), may hold values from -0.03125 to 0.03125
Outputs:
- left_new: bfloat16 [32768, 256], P(('modes', 'grp'))
- right_new: bfloat16 [32768, 256], P(('modes', 'grp'))
The draws below stay inside these ranges and needn't reach their ends.
All inputs are finite; a program needn't handle non-finite values.
Results may differ from the reference program's by a relative error of at most 0.0012.
Values sent between devices are 32-bit elements; how exact they have to be, the bound alone decides.
A program may use at most 64 MiB of HBM per device.

```python
import math
import jax
import jax.numpy as jnp
from jax import lax

R = 512
K = 256
ROWS = 32768


def levels(key, dims, pieces, low, high):
    level, own = 1.0, jax.random.fold_in(key, 6)
    for dim, shards_of in pieces:
        steps = jnp.exp(jax.random.uniform(jax.random.fold_in(own, dim), (shards_of,), jnp.float32, low / len(pieces), high / len(pieces)))
        level = level * jnp.repeat(steps, dims[dim] // shards_of).reshape([-1 if axis == dim else 1 for axis in range(len(dims))])
    return level


def centred(rng, dims, deviation, reach, pieces=(), dtype=jnp.bfloat16):
    result = jax.random.normal(rng, dims, jnp.float32) * deviation
    if len(pieces) > 0:
        result = levels(rng, dims, pieces, -0.22, 0.18) * result
    return jnp.clip(result, min=-reach, max=reach).astype(dtype)


def setup_inputs(seed: int = 0) -> dict:
    splits = jax.random.split(jax.random.key(seed), 4)
    left_core = centred(splits[0], (ROWS, R), 1.0, 6.0, ((0, 32),))
    right_core = centred(splits[1], (ROWS, R), 1.0, 6.0, ((0, 32),))
    gauss_core = centred(splits[2], (ROWS, K), ROWS ** -0.5, 0.03125, ((0, 32),))
    return {"left_core": left_core, "right_core": right_core, "gauss_core": gauss_core}


def reference(left_core, right_core, gauss_core):
    high = lax.Precision.HIGHEST
    sketch = lax.dot_general(right_core.astype(jnp.float32), gauss_core.astype(jnp.float32), (((0,), (0,)), ((), ())), preferred_element_type=jnp.float32)
    tall_sketch = jnp.dot(left_core.astype(jnp.float32), sketch, precision=high)
    gram = lax.dot_general(tall_sketch, tall_sketch, (((0,), (0,)), ((), ())), precision=high)
    chol_lower = jnp.linalg.cholesky(gram)
    q_trans = jax.scipy.linalg.solve_triangular(chol_lower, tall_sketch.T, lower=True)
    projected = jnp.dot(q_trans, left_core.astype(jnp.float32), precision=high)
    norm_scale = math.sqrt(ROWS)
    left_new = (q_trans.T * norm_scale).astype(jnp.bfloat16)
    right_new = jnp.dot(right_core.astype(jnp.float32), (projected / norm_scale).T, precision=high).astype(jnp.bfloat16)
    return (left_new, right_new)
```

```python
import functools
import math

import jax
import jax.numpy as jnp
from jax import lax
from jax.experimental import pallas as pl
from jax.experimental.pallas import tpu as pltpu
from jax.sharding import PartitionSpec as P

MESH = pl.DeviceIdType.MESH
F32 = jnp.float32
BF16 = jnp.bfloat16
B = 128
T = 8


def dot(a, b, dims, precision=None):
    return lax.dot_general(a, b, (dims, ((), ())), precision=precision, preferred_element_type=F32)


def block_list(rank, target):
    n, k = rank // B, target // B
    sketch = [(0, i, j) for i in range(n) for j in range(k)]
    gram = [(1, i, j) for i in range(n) for j in range(i, n)]
    return sketch + gram


def plan(rank, target, modes):
    devices = 2 * modes
    rows = len(block_list(rank, target)) * B
    tiles = -(-rows // (devices * T))
    a = -(-tiles // 2) * T
    b = tiles * T - a
    return a, b, (a + b) * devices


def reduce_kernel(modes, a, b, left, right, gauss, full, buf, r_core, ra1, rb1, ra2, rb2, rza, rzb, ssem, rsem, zsend, zrecv):
    nz = modes // 4
    m, c = lax.axis_index("modes"), lax.axis_index("grp")
    x, y, z = m % 2, (m // 2) % 2, m // 4
    core = (m, 1 - c)
    xp = (m + 1 - 2 * x, c)
    yp = (m + 2 - 4 * y, c)
    zs = [((z + k) % nz) for k in range(1, nz)]
    zp = [(x + 2 * y + 4 * t, c) for t in zs]

    barrier = pltpu.get_barrier_semaphore()
    partners = [core, xp, yp] + zp
    for p in partners:
        pl.semaphore_signal(barrier, inc=1, device_id=p, device_id_type=MESH)

    rank, target = right.shape[1], gauss.shape[1]
    n, kb = rank // B, target // B
    pos = 0
    for i in range(n):
        s = dot(right[:, i * B:(i + 1) * B], gauss[...], ((0,), (0,)))
        for j in range(kb):
            buf[pos * B:(pos + 1) * B, :] = s[:, j * B:(j + 1) * B]
            pos += 1
    for i in range(n):
        g = dot(left[:, i * B:(i + 1) * B], left[:, i * B:], ((0,), (0,)))
        for j in range(n - i):
            buf[pos * B:(pos + 1) * B, :] = g[:, j * B:(j + 1) * B]
            pos += 1
    total = buf.shape[0]
    if pos * B < total:
        buf[pos * B:, :] = jnp.zeros((total - pos * B, B), F32)

    pl.semaphore_wait(barrier, len(partners))

    half = total // 2
    qa, qb = nz * a, nz * b
    base_a = c * half
    base_b = base_a + 4 * qa

    def at(ref, start, size):
        return ref.at[pl.ds(pl.multiple_of(start, T), size), :]

    def send(src, dst, k, dev):
        cp = pltpu.make_async_remote_copy(
            src_ref=src, dst_ref=dst, send_sem=ssem.at[k], recv_sem=rsem.at[k], device_id=dev, device_id_type=MESH)
        cp.start()
        return cp

    def add(start, size, other):
        i = pl.ds(pl.multiple_of(start, T), size)
        buf[i, :] = buf[i, :] + other[...]

    cp = send(at(buf, (1 - c) * half, half), r_core, 0, core)
    cp.wait()
    add(base_a, half, r_core)

    a1, b1 = base_a + x * 2 * qa, base_b + y * 2 * qb
    cps = [send(at(buf, base_a + (1 - x) * 2 * qa, 2 * qa), ra1, 1, xp)]
    if b:
        cps.append(send(at(buf, base_b + (1 - y) * 2 * qb, 2 * qb), rb1, 2, yp))
    cps[0].wait()
    add(a1, 2 * qa, ra1)
    if b:
        cps[1].wait()
        add(b1, 2 * qb, rb1)
    a2, b2 = a1 + y * qa, b1 + x * qb
    cps = [send(at(buf, a1 + (1 - y) * qa, qa), ra2, 3, yp)]
    if b:
        cps.append(send(at(buf, b1 + (1 - x) * qb, qb), rb2, 4, xp))
    cps[0].wait()
    add(a2, qa, ra2)
    if b:
        cps[1].wait()
        add(b2, qb, rb2)

    def zsends(src, dst_a, dst_b, phase):
        cps = []
        for k in range(nz - 1):
            for part, base, size, dst in ((0, a2, a, dst_a), (1, b2, b, dst_b)):
                if not size:
                    continue
                where = zs[k] if phase == 0 else z
                source = at(src, base + where * size, size)
                target_ref = dst.at[k] if phase == 0 else source
                cp = pltpu.make_async_remote_copy(
                    src_ref=source, dst_ref=target_ref, send_sem=zsend.at[phase, part, k],
                    recv_sem=zrecv.at[phase, part, k], device_id=zp[k], device_id_type=MESH)
                cp.start()
                cps.append(cp)
        for cp in cps:
            cp.wait()

    zsends(buf, rza, rzb, 0)
    for base, size, got in ((a2, a, rza), (b2, b, rzb)):
        if size:
            i = pl.ds(pl.multiple_of(base + z * size, T), size)
            acc = buf[i, :]
            for k in range(nz - 1):
                acc = acc + got[k]
            full[i, :] = acc

    zsends(full, full, full, 1)
    cps = [send(at(full, a2, qa), at(full, a2, qa), 5, yp)]
    if b:
        cps.append(send(at(full, b2, qb), at(full, b2, qb), 6, xp))
    for cp in cps:
        cp.wait()
    cps = [send(at(full, a1, 2 * qa), at(full, a1, 2 * qa), 7, xp)]
    if b:
        cps.append(send(at(full, b1, 2 * qb), at(full, b1, 2 * qb), 8, yp))
    for cp in cps:
        cp.wait()
    send(at(full, base_a, half), at(full, base_a, half), 9, core).wait()


def reduced(left, right, gauss):
    modes = lax.axis_size("modes")
    a, b, total = plan(right.shape[1], gauss.shape[1], modes)
    nz = modes // 4
    bb = max(b, T)
    dma = pltpu.SemaphoreType.DMA
    return pl.pallas_call(
        functools.partial(reduce_kernel, modes, a, b),
        out_shape=jax.ShapeDtypeStruct((total, B), F32),
        in_specs=[pl.BlockSpec(memory_space=pltpu.VMEM)] * 3,
        out_specs=pl.BlockSpec(memory_space=pltpu.VMEM),
        scratch_shapes=[
            pltpu.VMEM((total, B), F32),
            pltpu.VMEM((total // 2, B), F32),
            pltpu.VMEM((2 * nz * a, B), F32),
            pltpu.VMEM((2 * nz * bb, B), F32),
            pltpu.VMEM((nz * a, B), F32),
            pltpu.VMEM((nz * bb, B), F32),
            pltpu.VMEM((nz - 1, a, B), F32),
            pltpu.VMEM((nz - 1, bb, B), F32),
            dma((10,)),
            dma((10,)),
            dma((2, 2, nz - 1)),
            dma((2, 2, nz - 1)),
        ],
        compiler_params=pltpu.CompilerParams(collective_id=0, has_side_effects=True, vmem_limit_bytes=40 << 20),
    )(left, right, gauss)


def factor_inverse(block, spl, rowbuf):
    n = B // T
    row = lax.broadcasted_iota(jnp.int32, (T, B), 0)
    lane = lax.broadcasted_iota(jnp.int32, (T, B), 1)
    A = [block[t * T:(t + 1) * T, :] for t in range(n)]
    M = [(row + t * T == lane).astype(F32) for t in range(n)]
    out = []
    for p in range(n):
        k0 = p * T
        for j in range(T):
            spl[p % 2, j] = jnp.broadcast_to(A[p][:, k0 + j:k0 + j + 1], (T, B))
        s = [[jnp.broadcast_to(spl[p % 2, j, i:i + 1, :], (T, B)) if j <= i else None for j in range(T)] for i in range(T)]
        w = [[None] * T for _ in range(T)]
        rs, rd = [], []
        for k in range(T):
            r = lax.rsqrt(s[k][k])
            rs.append(r)
            rd.append(r * r)
            for i in range(k + 1, T):
                w[i][k] = s[i][k] * rd[k]
            for j in range(k + 1, T):
                for i in range(j, T):
                    s[i][j] = s[i][j] - w[i][k] * s[j][k]
        rowbuf[p % 2, 0] = A[p]
        rowbuf[p % 2, 1] = M[p]
        xa = [jnp.broadcast_to(rowbuf[p % 2, 0, i:i + 1, :], (T, B)) for i in range(T)]
        xm = [jnp.broadcast_to(rowbuf[p % 2, 1, i:i + 1, :], (T, B)) for i in range(T)]
        for k in range(T):
            for i in range(k + 1, T):
                xa[i] = xa[i] - w[i][k] * xa[k]
                xm[i] = xm[i] - w[i][k] * xm[k]
        o = xm[0] * rs[0]
        for i in range(1, T):
            o = jnp.where(row == i, xm[i] * rs[i], o)
        out.append(o)
        if p + 1 == n:
            break
        va = [xa[i] * rd[i] for i in range(T)]
        vm = [xm[i] * rd[i] for i in range(T)]
        for k in range(T - 1, 0, -1):
            for i in range(k):
                va[i] = va[i] - w[k][i] * va[k]
                vm[i] = vm[i] - w[k][i] * vm[k]
        for t in range(p + 1, n):
            da = dm = None
            for j in range(T):
                cj = jnp.broadcast_to(A[t][:, k0 + j:k0 + j + 1], (T, B))
                da = cj * va[j] if da is None else da + cj * va[j]
                dm = cj * vm[j] if dm is None else dm + cj * vm[j]
            A[t] = A[t] - da
            M[t] = M[t] - dm
    return jnp.concatenate(out, axis=0)


def halves(v):
    hi = v.astype(BF16)
    return hi, (v - hi.astype(F32)).astype(BF16)


def solve_kernel(scale, full, left, right, left_new, right_new, sk, gm, spl, rowbuf):
    high = lax.Precision.HIGHEST
    rank, target = left.shape[1], left_new.shape[1]
    for pos, (kind, i, j) in enumerate(block_list(rank, target)):
        v = full[pos * B:(pos + 1) * B, :]
        if kind == 0:
            sk[j * B:(j + 1) * B, i * B:(i + 1) * B] = v.T
        else:
            gm[i * B:(i + 1) * B, j * B:(j + 1) * B] = v
            if i != j:
                gm[j * B:(j + 1) * B, i * B:(i + 1) * B] = v.T
    nn, nt = ((1,), (0,)), ((1,), (1,))
    st = sk[...]
    cross = dot(st, gm[...], nn, high)
    gram = dot(cross, st, nt, high)
    nb = target // B
    low, inv = [], []
    for r in range(nb):
        diag = gram[r * B:(r + 1) * B, r * B:(r + 1) * B]
        if r:
            prev = inv[0] if r == 1 else jnp.concatenate(inv, axis=0)
            lr = dot(gram[r * B:(r + 1) * B, :r * B], prev, nt, high)
            diag = diag - dot(lr, lr, nt, high)
        mi = factor_inverse(diag, spl, rowbuf)
        if r:
            rest = -dot(mi, dot(lr, prev, nn, high), nn, high)
            mi = jnp.concatenate([rest, mi], axis=1)
            inv = [jnp.concatenate([v, jnp.zeros((B, B), F32)], axis=1) for v in inv]
        inv.append(mi)
    inverse = inv[0] if nb == 1 else jnp.concatenate(inv, axis=0)
    wh, wl = halves(dot(inverse, st, nn, high) * scale)
    ph, plo = halves(dot(inverse, cross, nn, high) * (1.0 / scale))
    left_new[...] = (dot(left[...], wh, nt) + dot(left[...], wl, nt)).astype(BF16)
    right_new[...] = (dot(right[...], ph, nt) + dot(right[...], plo, nt)).astype(BF16)


def local(left_core, right_core, gauss_core):
    rows, rank = left_core.shape
    target = gauss_core.shape[1]
    devices = lax.axis_size("modes") * lax.axis_size("grp")
    full = reduced(left_core, right_core, gauss_core)
    out = jax.ShapeDtypeStruct((rows, target), BF16)
    return pl.pallas_call(
        functools.partial(solve_kernel, math.sqrt(rows * devices)),
        out_shape=(out, out),
        in_specs=[pl.BlockSpec(memory_space=pltpu.VMEM)] * 3,
        out_specs=(pl.BlockSpec(memory_space=pltpu.VMEM),) * 2,
        scratch_shapes=[
            pltpu.VMEM((target, rank), F32),
            pltpu.VMEM((rank, rank), F32),
            pltpu.VMEM((2, T, T, B), F32),
            pltpu.VMEM((2, 2, T, B), F32),
        ],
        compiler_params=pltpu.CompilerParams(vmem_limit_bytes=40 << 20),
    )(full, left_core, right_core)


def solution(mesh):
    spec = P(("modes", "grp"), None)
    return jax.shard_map(local, mesh=mesh, in_specs=(spec,) * 3, out_specs=(spec, spec), check_vma=False)
```

```python
import functools
import math

import jax
import jax.numpy as jnp
from jax import lax
from jax.experimental import pallas as pl
from jax.experimental.pallas import tpu as pltpu
from jax.sharding import PartitionSpec as P

MESH = pl.DeviceIdType.MESH
F32 = jnp.float32
BF16 = jnp.bfloat16
B = 128
T = 8
FULL_PARTS = 4
PARTS = 4


def dot(a, b, dims, precision=None):
    return lax.dot_general(a, b, (dims, ((), ())), precision=precision, preferred_element_type=F32)


def block_list(rank, target):
    n, k = rank // B, target // B
    sketch = [(0, i, j) for i in range(n) for j in range(k)]
    gram = [(1, i, j) for i in range(n) for j in range(i, n)]
    return sketch + gram


def plan(rank, target, modes):
    devices = 2 * modes
    unit = devices * T
    streams, row, counts = [], 0, []
    for kind in (0, 1):
        rows = B * sum(blk[0] == kind for blk in block_list(rank, target))
        units = -(-rows // unit)
        parts = [p for p in (units // 2, units - units // 2) if p]
        counts.append(len(parts))
        for index, part in enumerate(parts):
            streams.append((row, part * T, index == 0))
            row += part * unit
    return streams, counts, row


def first_rows(rank, target, modes):
    streams, counts, _ = plan(rank, target, modes)
    starts = (0, streams[counts[0]][0])
    seen, out = [0, 0], []
    for kind, _, _ in block_list(rank, target):
        out.append(starts[kind] + seen[kind] * B)
        seen[kind] += 1
    return out


def reduce_kernel(modes, left_hbm, right_hbm, gauss_hbm, out, left, right, gauss, buf, full, *rest):
    nz = modes // 4
    rank, target = right.shape[1], gauss.shape[1]
    streams, counts, total = plan(rank, target, modes)
    ns = len(streams)
    recvs = [rest[4 * i:4 * i + 4] for i in range(ns)]
    isem, osem, ssem, rsem, zsend, zrecv = rest[4 * ns:]
    m, c = lax.axis_index("modes"), lax.axis_index("grp")
    x, y, z = m % 2, (m // 2) % 2, m // 4
    core = (m, 1 - c)
    xp = (m + 1 - 2 * x, c)
    yp = (m + 2 - 4 * y, c)
    zs = [((z + k) % nz) for k in range(1, nz)]
    zp = [(x + 2 * y + 4 * t, c) for t in zs]

    rows = right.shape[0]
    loads = []
    for index, (src, dst) in enumerate(((right_hbm, right), (gauss_hbm, gauss), (left_hbm, left))):
        step = rows // PARTS
        for k in range(PARTS):
            cp = pltpu.make_async_copy(src.at[pl.ds(k * step, step), :], dst.at[pl.ds(k * step, step), :], isem.at[index, k])
            cp.start()
            loads.append(cp)

    barrier = pltpu.get_barrier_semaphore()
    partners = [core, xp, yp] + zp
    for p in partners:
        pl.semaphore_signal(barrier, inc=1, device_id=p, device_id_type=MESH)

    starts = first_rows(rank, target, modes)
    where = {blk: row for blk, row in zip(block_list(rank, target), starts)}

    def stream(index):
        off, p, x_first = streams[index]
        r0, r1, r2, rz = recvs[index]
        q = nz * p
        f, s = (x, y) if x_first else (y, x)
        fp, sp = (xp, yp) if x_first else (yp, xp)
        b0 = off + c * 4 * q
        b1 = b0 + f * 2 * q
        b2 = b1 + s * q

        def at(ref, start, size):
            return ref.at[pl.ds(pl.multiple_of(start, T), size), :]

        def send(src, dst, k, dev):
            cp = pltpu.make_async_remote_copy(
                src_ref=src, dst_ref=dst, send_sem=ssem.at[index, k], recv_sem=rsem.at[index, k],
                device_id=dev, device_id_type=MESH)
            cp.start()
            return cp

        def share(start, size, k, dev):
            return send(at(full, start, size), at(full, start, size), k, dev)

        def add(start, size, other):
            i = pl.ds(pl.multiple_of(start, T), size)
            buf[i, :] = buf[i, :] + other[...]

        cp = send(at(buf, off + (1 - c) * 4 * q, 4 * q), r0, 0, core)
        yield
        cp.wait()
        add(b0 + (1 - f) * 2 * q, 2 * q, r0.at[pl.ds(pl.multiple_of((1 - f) * 2 * q, T), 2 * q), :])
        cp = send(at(buf, b0 + (1 - f) * 2 * q, 2 * q), r1, 1, fp)
        add(b1, 2 * q, r0.at[pl.ds(pl.multiple_of(f * 2 * q, T), 2 * q), :])
        yield
        cp.wait()
        add(b1 + (1 - s) * q, q, r1.at[pl.ds(pl.multiple_of((1 - s) * q, T), q), :])
        cp = send(at(buf, b1 + (1 - s) * q, q), r2, 2, sp)
        add(b2, q, r1.at[pl.ds(pl.multiple_of(s * q, T), q), :])
        yield
        cp.wait()
        add(b2, q, r2)
        cps = []
        for k in range(nz - 1):
            cp = pltpu.make_async_remote_copy(
                src_ref=at(buf, b2 + zs[k] * p, p), dst_ref=rz.at[k], send_sem=zsend.at[index, 0, k],
                recv_sem=zrecv.at[index, 0, k], device_id=zp[k], device_id_type=MESH)
            cp.start()
            cps.append(cp)
        yield
        piece = pl.ds(pl.multiple_of(b2 + z * p, T), p)
        acc = buf[piece, :]
        for k in range(nz - 1):
            cps[k].wait()
            acc = acc + rz[k]
        full[piece, :] = acc
        cps = []
        for k in range(nz - 1):
            cp = pltpu.make_async_remote_copy(
                src_ref=full.at[piece, :], dst_ref=full.at[piece, :], send_sem=zsend.at[index, 1, k],
                recv_sem=zrecv.at[index, 1, k], device_id=zp[k], device_id_type=MESH)
            cp.start()
            cps.append(cp)
        yield
        for cp in cps:
            cp.wait()
        c3 = share(b2, q, 3, sp)
        c4 = share(b2, q, 4, fp)
        c5 = share(b2, q, 5, core)
        yield
        c3.wait()
        o2 = b1 + (1 - s) * q
        c6 = share(o2, q, 6, fp)
        c7 = share(o2, q, 7, core)
        yield
        c4.wait()
        c8 = share(b0 + (1 - f) * 2 * q + s * q, q, 8, core)
        yield
        c6.wait()
        c9 = share(b0 + (1 - f) * 2 * q + (1 - s) * q, q, 9, core)
        mine = pltpu.make_async_copy(at(full, b0, 4 * q), at(out, b0, 4 * q), osem.at[index, 0])
        mine.start()
        yield
        for cp in (c5, c7, c8, c9):
            cp.wait()
        theirs = off + (1 - c) * 4 * q
        other = pltpu.make_async_copy(at(full, theirs, 4 * q), at(out, theirs, 4 * q), osem.at[index, 1])
        other.start()
        yield
        mine.wait()
        other.wait()

    for cp in loads[:2 * PARTS]:
        cp.wait()
    sketch = dot(right[...], gauss[...], ((0,), (0,)))
    for (kind, i, j), row in where.items():
        if kind == 0:
            buf[row:row + B, :] = sketch[i * B:(i + 1) * B, j * B:(j + 1) * B]
    end = max(starts) + B
    gram_start = streams[counts[0]][0]
    pad = B * sum(k == 0 for k, _, _ in where)
    if pad < gram_start:
        buf[pad:gram_start, :] = jnp.zeros((gram_start - pad, B), F32)
    if end < total:
        buf[end:, :] = jnp.zeros((total - end, B), F32)
    pl.semaphore_wait(barrier, len(partners))

    active = [stream(i) for i in range(counts[0])]
    for g in active:
        next(g)
    for cp in loads[2 * PARTS:]:
        cp.wait()
    step = 2 * B if rank % (2 * B) == 0 else B
    for r in range(0, rank, step):
        g = dot(left[:, r:r + step], left[:, r:], ((0,), (0,)))
        for i in range(r // B, (r + step) // B):
            for j in range(i, rank // B):
                row = where[(1, i, j)]
                buf[row:row + B, :] = g[i * B - r:(i + 1) * B - r, j * B - r:(j + 1) * B - r]
    late = [stream(counts[0] + i) for i in range(counts[1])]
    for g in late:
        next(g)
    active = active + late
    while active:
        active = [g for g in active if next(g, 0) != 0]


def reduced(left, right, gauss):
    modes = lax.axis_size("modes")
    rows, rank = right.shape
    target = gauss.shape[1]
    streams, _, total = plan(rank, target, modes)
    nz = modes // 4
    dma = pltpu.SemaphoreType.DMA
    landing = []
    for _, p, _ in streams:
        q = nz * p
        landing += [pltpu.VMEM((4 * q, B), F32), pltpu.VMEM((2 * q, B), F32), pltpu.VMEM((q, B), F32), pltpu.VMEM((nz - 1, p, B), F32)]
    return pl.pallas_call(
        functools.partial(reduce_kernel, modes),
        out_shape=jax.ShapeDtypeStruct((total, B), F32),
        in_specs=[pl.BlockSpec(memory_space=pl.ANY)] * 3,
        out_specs=pl.BlockSpec(memory_space=pl.ANY),
        scratch_shapes=[
            pltpu.VMEM((rows, rank), BF16),
            pltpu.VMEM((rows, rank), BF16),
            pltpu.VMEM((rows, target), BF16),
            pltpu.VMEM((total, B), F32),
            pltpu.VMEM((total, B), F32),
            *landing,
            dma((3, PARTS)),
            dma((len(streams), 2)),
            dma((len(streams), 10)),
            dma((len(streams), 10)),
            dma((len(streams), 2, nz - 1)),
            dma((len(streams), 2, nz - 1)),
        ],
        compiler_params=pltpu.CompilerParams(collective_id=0, has_side_effects=True, vmem_limit_bytes=61 << 20),
    )(left, right, gauss)


def factor_inverse(block, spl, rowbuf):
    n = B // T
    row = lax.broadcasted_iota(jnp.int32, (T, B), 0)
    lane = lax.broadcasted_iota(jnp.int32, (T, B), 1)
    A = [block[t * T:(t + 1) * T, :] for t in range(n)]
    M = [(row + t * T == lane).astype(F32) for t in range(n)]
    out = []
    for p in range(n):
        k0 = p * T
        for j in range(T):
            spl[p % 2, j] = jnp.broadcast_to(A[p][:, k0 + j:k0 + j + 1], (T, B))
        s = [[jnp.broadcast_to(spl[p % 2, j, i:i + 1, :], (T, B)) if j <= i else None for j in range(T)] for i in range(T)]
        w = [[None] * T for _ in range(T)]
        rs, rd = [], []
        for k in range(T):
            r = lax.rsqrt(s[k][k])
            rs.append(r)
            rd.append(r * r)
            for i in range(k + 1, T):
                w[i][k] = s[i][k] * rd[k]
            for j in range(k + 1, T):
                for i in range(j, T):
                    s[i][j] = s[i][j] - w[i][k] * s[j][k]
        rowbuf[p % 2, 0] = A[p]
        rowbuf[p % 2, 1] = M[p]
        xa = [jnp.broadcast_to(rowbuf[p % 2, 0, i:i + 1, :], (T, B)) for i in range(T)]
        xm = [jnp.broadcast_to(rowbuf[p % 2, 1, i:i + 1, :], (T, B)) for i in range(T)]
        for k in range(T):
            for i in range(k + 1, T):
                xa[i] = xa[i] - w[i][k] * xa[k]
                xm[i] = xm[i] - w[i][k] * xm[k]
        o = xm[0] * rs[0]
        for i in range(1, T):
            o = jnp.where(row == i, xm[i] * rs[i], o)
        out.append(o)
        if p + 1 == n:
            break
        va = [xa[i] * rd[i] for i in range(T)]
        vm = [xm[i] * rd[i] for i in range(T)]
        for k in range(T - 1, 0, -1):
            for i in range(k):
                va[i] = va[i] - w[k][i] * va[k]
                vm[i] = vm[i] - w[k][i] * vm[k]
        for t in range(p + 1, n):
            da = dm = None
            for j in range(T):
                cj = jnp.broadcast_to(A[t][:, k0 + j:k0 + j + 1], (T, B))
                da = cj * va[j] if da is None else da + cj * va[j]
                dm = cj * vm[j] if dm is None else dm + cj * vm[j]
            A[t] = A[t] - da
            M[t] = M[t] - dm
    return jnp.concatenate(out, axis=0)


def halves(v):
    hi = v.astype(BF16)
    return hi, (v - hi.astype(F32)).astype(BF16)


def solve_kernel(scale, modes, full_hbm, left_hbm, right_hbm, left_new, right_new, full, left, right, lout, rout, sk, gm, spl, rowbuf, fsem, isem, osem):
    high = lax.Precision.HIGHEST
    rows, rank, target = left.shape[0], left.shape[1], lout.shape[1]
    step = rows // PARTS
    parts = [pl.ds(k * step, step) for k in range(PARTS)]
    blocks = list(zip(block_list(rank, target), first_rows(rank, target, modes)))
    chunk = full.shape[0] // FULL_PARTS
    gets = []
    for k in range(FULL_PARTS):
        cp = pltpu.make_async_copy(full_hbm.at[pl.ds(k * chunk, chunk), :], full.at[pl.ds(k * chunk, chunk), :], fsem.at[k])
        cp.start()
        gets.append(cp)
    loads = []
    for index, (src, dst) in enumerate(((left_hbm, left), (right_hbm, right))):
        for k, part in enumerate(parts):
            cp = pltpu.make_async_copy(src.at[part, :], dst.at[part, :], isem.at[index, k])
            cp.start()
            loads.append(cp)
    for cp in gets:
        cp.wait()
    for (kind, i, j), pos in blocks:
        v = full[pos:pos + B, :]
        if kind == 0:
            sk[j * B:(j + 1) * B, i * B:(i + 1) * B] = v.T
        else:
            gm[i * B:(i + 1) * B, j * B:(j + 1) * B] = v
            if i != j:
                gm[j * B:(j + 1) * B, i * B:(i + 1) * B] = v.T
    nn, nt = ((1,), (0,)), ((1,), (1,))
    st = sk[...]
    cross = dot(st, gm[...], nn, high)
    gram = dot(cross, st, nt, high)
    nb = target // B
    low, inv = [], []
    for r in range(nb):
        diag = gram[r * B:(r + 1) * B, r * B:(r + 1) * B]
        if r:
            prev = inv[0] if r == 1 else jnp.concatenate(inv, axis=0)
            lr = dot(gram[r * B:(r + 1) * B, :r * B], prev, nt, high)
            diag = diag - dot(lr, lr, nt, high)
        mi = factor_inverse(diag, spl, rowbuf)
        if r:
            rest = -dot(mi, dot(lr, prev, nn, high), nn, high)
            mi = jnp.concatenate([rest, mi], axis=1)
            inv = [jnp.concatenate([v, jnp.zeros((B, B), F32)], axis=1) for v in inv]
        inv.append(mi)
    inverse = inv[0] if nb == 1 else jnp.concatenate(inv, axis=0)
    wh, wl = halves(dot(inverse, st, nn, high) * scale)
    ph, plo = halves(dot(inverse, cross, nn, high) * (1.0 / scale))
    for cp in loads:
        cp.wait()
    stores = []
    for index, (src, hi, lo, out, dst) in enumerate(((left, wh, wl, lout, left_new), (right, ph, plo, rout, right_new))):
        for k, part in enumerate(parts):
            v = src[part, :]
            out[part, :] = (dot(v, hi, nt) + dot(v, lo, nt)).astype(BF16)
            cp = pltpu.make_async_copy(out.at[part, :], dst.at[part, :], osem.at[index, k])
            cp.start()
            stores.append(cp)
    for cp in stores:
        cp.wait()


def local(left_core, right_core, gauss_core):
    rows, rank = left_core.shape
    target = gauss_core.shape[1]
    devices = lax.axis_size("modes") * lax.axis_size("grp")
    full = reduced(left_core, right_core, gauss_core)
    out = jax.ShapeDtypeStruct((rows, target), BF16)
    return pl.pallas_call(
        functools.partial(solve_kernel, math.sqrt(rows * devices), lax.axis_size("modes")),
        out_shape=(out, out),
        in_specs=[pl.BlockSpec(memory_space=pl.ANY)] * 3,
        out_specs=(pl.BlockSpec(memory_space=pl.ANY),) * 2,
        scratch_shapes=[
            pltpu.VMEM(full.shape, F32),
            pltpu.VMEM((rows, rank), BF16),
            pltpu.VMEM((rows, rank), BF16),
            pltpu.VMEM((rows, target), BF16),
            pltpu.VMEM((rows, target), BF16),
            pltpu.VMEM((target, rank), F32),
            pltpu.VMEM((rank, rank), F32),
            pltpu.VMEM((2, T, T, B), F32),
            pltpu.VMEM((2, 2, T, B), F32),
            pltpu.SemaphoreType.DMA((FULL_PARTS,)),
            pltpu.SemaphoreType.DMA((2, PARTS)),
            pltpu.SemaphoreType.DMA((2, PARTS)),
        ],
        compiler_params=pltpu.CompilerParams(vmem_limit_bytes=61 << 20),
    )(full, left_core, right_core)


def solution(mesh):
    spec = P(("modes", "grp"), None)
    return jax.shard_map(local, mesh=mesh, in_specs=(spec,) * 3, out_specs=(spec, spec), check_vma=False)
```

```python
import functools
import math

import jax
import jax.numpy as jnp
from jax import lax
from jax.experimental import pallas as pl
from jax.experimental.pallas import tpu as pltpu
from jax.sharding import PartitionSpec as P

MESH = pl.DeviceIdType.MESH
F32 = jnp.float32
BF16 = jnp.bfloat16
B = 128
T = 8
FULL_PARTS = 4
PARTS = 4


def dot(a, b, dims, precision=None):
    return lax.dot_general(a, b, (dims, ((), ())), precision=precision, preferred_element_type=F32)


def block_list(rank, target):
    n, k = rank // B, target // B
    sketch = [(0, i, j) for i in range(n) for j in range(k)]
    gram = [(1, i, j) for i in range(n) for j in range(i, n)]
    return sketch + gram


ORDERS = (((0, 1, 2), (1, 2, 0)), ((2, 0, 1), (0, 1, 2), (1, 0, 2)))


def plan(rank, target, modes):
    devices = 2 * modes
    unit = devices * T
    streams, row, counts = [], 0, []
    for kind in (0, 1):
        rows = B * sum(blk[0] == kind for blk in block_list(rank, target))
        units = -(-rows // unit)
        ways = len(ORDERS[kind])
        count = 0
        for index in range(ways):
            part = (units + ways - 1 - index) // ways
            if part:
                streams.append((row, part * T, ORDERS[kind][index] + tuple(range(3, modes.bit_length() - 1))))
                row += part * unit
                count += 1
        counts.append(count)
    return streams, counts, row


def first_rows(rank, target, modes):
    streams, counts, _ = plan(rank, target, modes)
    starts = (0, streams[counts[0]][0])
    seen, out = [0, 0], []
    for kind, _, _ in block_list(rank, target):
        out.append(starts[kind] + seen[kind] * B)
        seen[kind] += 1
    return out


def reduce_kernel(modes, left_hbm, right_hbm, gauss_hbm, out, left, right, gauss, buf, full, *rest):
    rank, target = right.shape[1], gauss.shape[1]
    streams, counts, total = plan(rank, target, modes)
    ns = len(streams)
    landings = rest[:ns]
    isem, osem, ssem, rsem = rest[ns:]
    m, c = lax.axis_index("modes"), lax.axis_index("grp")
    core = (m, 1 - c)
    bits = [(m // 2**k) % 2 for k in range(modes.bit_length() - 1)]
    across = [(m + (1 - 2 * v) * 2**k, c) for k, v in enumerate(bits)]

    rows = right.shape[0]
    loads = []
    for index, (src, dst) in enumerate(((right_hbm, right), (gauss_hbm, gauss), (left_hbm, left))):
        step = rows // PARTS
        for k in range(PARTS):
            cp = pltpu.make_async_copy(src.at[pl.ds(k * step, step), :], dst.at[pl.ds(k * step, step), :], isem.at[index, k])
            cp.start()
            loads.append(cp)

    barrier = pltpu.get_barrier_semaphore()
    partners = [core] + across
    for p in partners:
        pl.semaphore_signal(barrier, inc=1, device_id=p, device_id_type=MESH)

    starts = first_rows(rank, target, modes)
    where = {blk: row for blk, row in zip(block_list(rank, target), starts)}

    sems = ssem.shape[1]

    def stream(index):
        off, p, order = streams[index]
        landing = landings[index]
        count = iter(range(sems))

        def at(ref, start, size):
            return ref.at[pl.ds(pl.multiple_of(start, T), size), :]

        def send(src, dst, dev):
            k = next(count)
            cp = pltpu.make_async_remote_copy(
                src_ref=src, dst_ref=dst, send_sem=ssem.at[index, k], recv_sem=rsem.at[index, k],
                device_id=dev, device_id_type=MESH)
            cp.start()
            return cp

        def share(start, size, dev):
            return send(at(full, start, size), at(full, start, size), dev)

        size, base, free = 2 * p * modes, off, 0
        for step, (v, dev) in enumerate([(c, core)] + [(bits[k], across[k]) for k in order]):
            size //= 2
            got = landing.at[pl.ds(free, size), :]
            free += size
            cp = send(at(buf, base + (1 - v) * size, size), got, dev)
            yield
            cp.wait()
            base = base + v * size
            i = pl.ds(pl.multiple_of(base, T), size)
            if step < len(order):
                buf[i, :] = buf[i, :] + got[...]
            else:
                full[i, :] = buf[i, :] + got[...]

        shared = [share(base, size, core)]
        for k in reversed(order):
            v = bits[k]
            cp = share(base, size, across[k])
            yield
            cp.wait()
            shared.append(share(base + (1 - 2 * v) * size, size, core))
            base = base - v * size
            size *= 2
        mine = pltpu.make_async_copy(at(full, base, size), at(out, base, size), osem.at[index, 0])
        mine.start()
        yield
        for cp in shared:
            cp.wait()
        theirs = off + (1 - c) * size
        other = pltpu.make_async_copy(at(full, theirs, size), at(out, theirs, size), osem.at[index, 1])
        other.start()
        yield
        mine.wait()
        other.wait()

    for cp in loads[:2 * PARTS]:
        cp.wait()
    sketch = dot(right[...], gauss[...], ((0,), (0,)))
    for (kind, i, j), row in where.items():
        if kind == 0:
            buf[row:row + B, :] = sketch[i * B:(i + 1) * B, j * B:(j + 1) * B]
    end = max(starts) + B
    gram_start = streams[counts[0]][0]
    pad = B * sum(k == 0 for k, _, _ in where)
    if pad < gram_start:
        buf[pad:gram_start, :] = jnp.zeros((gram_start - pad, B), F32)
    if end < total:
        buf[end:, :] = jnp.zeros((total - end, B), F32)
    pl.semaphore_wait(barrier, len(partners))

    active = [stream(i) for i in range(counts[0])]
    for g in active:
        next(g)
    for cp in loads[2 * PARTS:]:
        cp.wait()
    step = 2 * B if rank % (2 * B) == 0 else B
    for r in range(0, rank, step):
        g = dot(left[:, r:r + step], left[:, r:], ((0,), (0,)))
        for i in range(r // B, (r + step) // B):
            for j in range(i, rank // B):
                row = where[(1, i, j)]
                buf[row:row + B, :] = g[i * B - r:(i + 1) * B - r, j * B - r:(j + 1) * B - r]
    late = [stream(counts[0] + i) for i in range(counts[1])]
    for g in late:
        next(g)
    active = active + late
    while active:
        active = [g for g in active if next(g, 0) != 0]


def reduced(left, right, gauss):
    modes = lax.axis_size("modes")
    rows, rank = right.shape
    target = gauss.shape[1]
    streams, _, total = plan(rank, target, modes)
    dma = pltpu.SemaphoreType.DMA
    landing = [pltpu.VMEM((2 * p * modes, B), F32) for _, p, _ in streams]
    sems = 3 * modes.bit_length()
    return pl.pallas_call(
        functools.partial(reduce_kernel, modes),
        out_shape=jax.ShapeDtypeStruct((total, B), F32),
        in_specs=[pl.BlockSpec(memory_space=pl.ANY)] * 3,
        out_specs=pl.BlockSpec(memory_space=pl.ANY),
        scratch_shapes=[
            pltpu.VMEM((rows, rank), BF16),
            pltpu.VMEM((rows, rank), BF16),
            pltpu.VMEM((rows, target), BF16),
            pltpu.VMEM((total, B), F32),
            pltpu.VMEM((total, B), F32),
            *landing,
            dma((3, PARTS)),
            dma((len(streams), 2)),
            dma((len(streams), sems)),
            dma((len(streams), sems)),
        ],
        compiler_params=pltpu.CompilerParams(collective_id=0, has_side_effects=True, vmem_limit_bytes=61 << 20),
    )(left, right, gauss)


def factor_inverse(block, spl, rowbuf):
    n = B // T
    row = lax.broadcasted_iota(jnp.int32, (T, B), 0)
    lane = lax.broadcasted_iota(jnp.int32, (T, B), 1)
    A = [block[t * T:(t + 1) * T, :] for t in range(n)]
    M = [(row + t * T == lane).astype(F32) for t in range(n)]
    out = []
    for p in range(n):
        k0 = p * T
        for j in range(T):
            spl[p % 2, j] = jnp.broadcast_to(A[p][:, k0 + j:k0 + j + 1], (T, B))
        s = [[jnp.broadcast_to(spl[p % 2, j, i:i + 1, :], (T, B)) if j <= i else None for j in range(T)] for i in range(T)]
        w = [[None] * T for _ in range(T)]
        rs, rd = [], []
        for k in range(T):
            r = lax.rsqrt(s[k][k])
            rs.append(r)
            rd.append(r * r)
            for i in range(k + 1, T):
                w[i][k] = s[i][k] * rd[k]
            for j in range(k + 1, T):
                for i in range(j, T):
                    s[i][j] = s[i][j] - w[i][k] * s[j][k]
        rowbuf[p % 2, 0] = A[p]
        rowbuf[p % 2, 1] = M[p]
        xa = [jnp.broadcast_to(rowbuf[p % 2, 0, i:i + 1, :], (T, B)) for i in range(T)]
        xm = [jnp.broadcast_to(rowbuf[p % 2, 1, i:i + 1, :], (T, B)) for i in range(T)]
        for k in range(T):
            for i in range(k + 1, T):
                xa[i] = xa[i] - w[i][k] * xa[k]
                xm[i] = xm[i] - w[i][k] * xm[k]
        o = xm[0] * rs[0]
        for i in range(1, T):
            o = jnp.where(row == i, xm[i] * rs[i], o)
        out.append(o)
        if p + 1 == n:
            break
        va = [xa[i] * rd[i] for i in range(T)]
        vm = [xm[i] * rd[i] for i in range(T)]
        for k in range(T - 1, 0, -1):
            for i in range(k):
                va[i] = va[i] - w[k][i] * va[k]
                vm[i] = vm[i] - w[k][i] * vm[k]
        for t in range(p + 1, n):
            da = dm = None
            for j in range(T):
                cj = jnp.broadcast_to(A[t][:, k0 + j:k0 + j + 1], (T, B))
                da = cj * va[j] if da is None else da + cj * va[j]
                dm = cj * vm[j] if dm is None else dm + cj * vm[j]
            A[t] = A[t] - da
            M[t] = M[t] - dm
    return jnp.concatenate(out, axis=0)


def halves(v):
    hi = v.astype(BF16)
    return hi, (v - hi.astype(F32)).astype(BF16)


def product(a, b):
    ah, al = halves(a)
    bh, bl = halves(b)
    nn = ((1,), (0,))
    return dot(ah, bh, nn) + (dot(ah, bl, nn) + dot(al, bh, nn))


def solve_kernel(scale, modes, full_hbm, left_hbm, right_hbm, left_new, right_new, full, left, right, lout, rout, sk, gm, spl, rowbuf, fsem, isem, osem):
    high = lax.Precision.HIGHEST
    rows, rank, target = left.shape[0], left.shape[1], lout.shape[1]
    step = rows // PARTS
    parts = [pl.ds(k * step, step) for k in range(PARTS)]
    blocks = list(zip(block_list(rank, target), first_rows(rank, target, modes)))
    chunk = full.shape[0] // FULL_PARTS
    gets = []
    for k in range(FULL_PARTS):
        cp = pltpu.make_async_copy(full_hbm.at[pl.ds(k * chunk, chunk), :], full.at[pl.ds(k * chunk, chunk), :], fsem.at[k])
        cp.start()
        gets.append(cp)
    for cp in gets:
        cp.wait()
    loads = []
    for index, (src, dst) in enumerate(((left_hbm, left), (right_hbm, right))):
        for k, part in enumerate(parts):
            cp = pltpu.make_async_copy(src.at[part, :], dst.at[part, :], isem.at[index, k])
            cp.start()
            loads.append(cp)
    for (kind, i, j), pos in blocks:
        v = full[pos:pos + B, :]
        if kind == 0:
            sk[j * B:(j + 1) * B, i * B:(i + 1) * B] = v.T
        else:
            gm[i * B:(i + 1) * B, j * B:(j + 1) * B] = v
            if i != j:
                gm[j * B:(j + 1) * B, i * B:(i + 1) * B] = v.T
    nn, nt = ((1,), (0,)), ((1,), (1,))
    st = sk[...]
    cross = dot(st, gm[...], nn, high)
    gram = dot(cross, st, nt, high)
    nb = target // B
    low, inv = [], []
    for r in range(nb):
        diag = gram[r * B:(r + 1) * B, r * B:(r + 1) * B]
        if r:
            prev = inv[0] if r == 1 else jnp.concatenate(inv, axis=0)
            lr = dot(gram[r * B:(r + 1) * B, :r * B], prev, nt, high)
            diag = diag - dot(lr, lr, nt, high)
        mi = factor_inverse(diag, spl, rowbuf)
        if r:
            rest = -dot(mi, dot(lr, prev, nn, high), nn, high)
            mi = jnp.concatenate([rest, mi], axis=1)
            inv = [jnp.concatenate([v, jnp.zeros((B, B), F32)], axis=1) for v in inv]
        inv.append(mi)
    inverse = inv[0] if nb == 1 else jnp.concatenate(inv, axis=0)
    wh, wl = halves(product(inverse, st) * scale)
    ph, plo = halves(product(inverse, cross) * (1.0 / scale))
    for cp in loads:
        cp.wait()
    stores = []
    for index, (src, hi, lo, out, dst) in enumerate(((left, wh, wl, lout, left_new), (right, ph, plo, rout, right_new))):
        for k, part in enumerate(parts):
            v = src[part, :]
            out[part, :] = (dot(v, hi, nt) + dot(v, lo, nt)).astype(BF16)
            cp = pltpu.make_async_copy(out.at[part, :], dst.at[part, :], osem.at[index, k])
            cp.start()
            stores.append(cp)
    for cp in stores:
        cp.wait()


def local(left_core, right_core, gauss_core):
    rows, rank = left_core.shape
    target = gauss_core.shape[1]
    devices = lax.axis_size("modes") * lax.axis_size("grp")
    full = reduced(left_core, right_core, gauss_core)
    out = jax.ShapeDtypeStruct((rows, target), BF16)
    return pl.pallas_call(
        functools.partial(solve_kernel, math.sqrt(rows * devices), lax.axis_size("modes")),
        out_shape=(out, out),
        in_specs=[pl.BlockSpec(memory_space=pl.ANY)] * 3,
        out_specs=(pl.BlockSpec(memory_space=pl.ANY),) * 2,
        scratch_shapes=[
            pltpu.VMEM(full.shape, F32),
            pltpu.VMEM((rows, rank), BF16),
            pltpu.VMEM((rows, rank), BF16),
            pltpu.VMEM((rows, target), BF16),
            pltpu.VMEM((rows, target), BF16),
            pltpu.VMEM((target, rank), F32),
            pltpu.VMEM((rank, rank), F32),
            pltpu.VMEM((2, T, T, B), F32),
            pltpu.VMEM((2, 2, T, B), F32),
            pltpu.SemaphoreType.DMA((FULL_PARTS,)),
            pltpu.SemaphoreType.DMA((2, PARTS)),
            pltpu.SemaphoreType.DMA((2, PARTS)),
        ],
        compiler_params=pltpu.CompilerParams(vmem_limit_bytes=61 << 20),
    )(full, left_core, right_core)


def solution(mesh):
    spec = P(("modes", "grp"), None)
    return jax.shard_map(local, mesh=mesh, in_specs=(spec,) * 3, out_specs=(spec, spec), check_vma=False)
```

```python
import functools
import math

import jax
import jax.numpy as jnp
from jax import lax
from jax.experimental import pallas as pl
from jax.experimental.pallas import tpu as pltpu
from jax.sharding import PartitionSpec as P

MESH = pl.DeviceIdType.MESH
F32 = jnp.float32
BF16 = jnp.bfloat16
B = 128
T = 8
FULL_PARTS = 4
PARTS = 4


def dot(a, b, dims, precision=None):
    return lax.dot_general(a, b, (dims, ((), ())), precision=precision, preferred_element_type=F32)


def block_list(rank, target):
    n, k = rank // B, target // B
    sketch = [(0, i, j) for i in range(n) for j in range(k)]
    gram = [(1, i, j) for i in range(n) for j in range(i, n)]
    return sketch + gram


def plan(rank, target, modes):
    devices = 2 * modes
    unit = devices * T
    streams, row, counts = [], 0, []
    for kind in (0, 1):
        rows = B * sum(blk[0] == kind for blk in block_list(rank, target))
        units = -(-rows // unit)
        parts = [p for p in (units // 2, units - units // 2) if p]
        counts.append(len(parts))
        for index, part in enumerate(parts):
            streams.append((row, part * T, index == 0))
            row += part * unit
    return streams, counts, row


def first_rows(rank, target, modes):
    streams, counts, _ = plan(rank, target, modes)
    starts = (0, streams[counts[0]][0])
    seen, out = [0, 0], []
    for kind, _, _ in block_list(rank, target):
        out.append(starts[kind] + seen[kind] * B)
        seen[kind] += 1
    return out


def reduce_kernel(modes, left_hbm, right_hbm, gauss_hbm, out, left, right, gauss, buf, full, *rest):
    nz = modes // 4
    rank, target = right.shape[1], gauss.shape[1]
    streams, counts, total = plan(rank, target, modes)
    ns = len(streams)
    recvs = [rest[4 * i:4 * i + 4] for i in range(ns)]
    isem, osem, ssem, rsem, zsend, zrecv = rest[4 * ns:]
    m, c = lax.axis_index("modes"), lax.axis_index("grp")
    x, y, z = m % 2, (m // 2) % 2, m // 4
    core = (m, 1 - c)
    xp = (m + 1 - 2 * x, c)
    yp = (m + 2 - 4 * y, c)
    zs = [((z + k) % nz) for k in range(1, nz)]
    zp = [(x + 2 * y + 4 * t, c) for t in zs]

    rows = right.shape[0]
    loads = []
    for index, (src, dst) in enumerate(((right_hbm, right), (gauss_hbm, gauss), (left_hbm, left))):
        step = rows // PARTS
        for k in range(PARTS):
            cp = pltpu.make_async_copy(src.at[pl.ds(k * step, step), :], dst.at[pl.ds(k * step, step), :], isem.at[index, k])
            cp.start()
            loads.append(cp)

    barrier = pltpu.get_barrier_semaphore()
    partners = [core, xp, yp] + zp
    for p in partners:
        pl.semaphore_signal(barrier, inc=1, device_id=p, device_id_type=MESH)

    starts = first_rows(rank, target, modes)
    where = {blk: row for blk, row in zip(block_list(rank, target), starts)}

    def stream(index):
        off, p, x_first = streams[index]
        r0, r1, r2, rz = recvs[index]
        q = nz * p
        f, s = (x, y) if x_first else (y, x)
        fp, sp = (xp, yp) if x_first else (yp, xp)
        b0 = off + c * 4 * q
        b1 = b0 + f * 2 * q
        b2 = b1 + s * q

        def at(ref, start, size):
            return ref.at[pl.ds(pl.multiple_of(start, T), size), :]

        def send(src, dst, k, dev):
            cp = pltpu.make_async_remote_copy(
                src_ref=src, dst_ref=dst, send_sem=ssem.at[index, k], recv_sem=rsem.at[index, k],
                device_id=dev, device_id_type=MESH)
            cp.start()
            return cp

        def share(start, size, k, dev):
            return send(at(full, start, size), at(full, start, size), k, dev)

        def add(start, size, other):
            i = pl.ds(pl.multiple_of(start, T), size)
            buf[i, :] = buf[i, :] + other[...]

        cp = send(at(buf, off + (1 - c) * 4 * q, 4 * q), r0, 0, core)
        yield
        cp.wait()
        add(b0 + (1 - f) * 2 * q, 2 * q, r0.at[pl.ds(pl.multiple_of((1 - f) * 2 * q, T), 2 * q), :])
        cp = send(at(buf, b0 + (1 - f) * 2 * q, 2 * q), r1, 1, fp)
        add(b1, 2 * q, r0.at[pl.ds(pl.multiple_of(f * 2 * q, T), 2 * q), :])
        yield
        cp.wait()
        add(b1 + (1 - s) * q, q, r1.at[pl.ds(pl.multiple_of((1 - s) * q, T), q), :])
        cp = send(at(buf, b1 + (1 - s) * q, q), r2, 2, sp)
        add(b2, q, r1.at[pl.ds(pl.multiple_of(s * q, T), q), :])
        yield
        cp.wait()
        add(b2, q, r2)
        cps = []
        for k in range(nz - 1):
            cp = pltpu.make_async_remote_copy(
                src_ref=at(buf, b2 + zs[k] * p, p), dst_ref=rz.at[k], send_sem=zsend.at[index, 0, k],
                recv_sem=zrecv.at[index, 0, k], device_id=zp[k], device_id_type=MESH)
            cp.start()
            cps.append(cp)
        yield
        piece = pl.ds(pl.multiple_of(b2 + z * p, T), p)
        acc = buf[piece, :]
        for k in range(nz - 1):
            cps[k].wait()
            acc = acc + rz[k]
        full[piece, :] = acc
        cps = []
        for k in range(nz - 1):
            cp = pltpu.make_async_remote_copy(
                src_ref=full.at[piece, :], dst_ref=full.at[piece, :], send_sem=zsend.at[index, 1, k],
                recv_sem=zrecv.at[index, 1, k], device_id=zp[k], device_id_type=MESH)
            cp.start()
            cps.append(cp)
        yield
        for cp in cps:
            cp.wait()
        c3 = share(b2, q, 3, sp)
        c4 = share(b2, q, 4, fp)
        c5 = share(b2, q, 5, core)
        yield
        c3.wait()
        o2 = b1 + (1 - s) * q
        c6 = share(o2, q, 6, fp)
        c7 = share(o2, q, 7, core)
        yield
        c4.wait()
        c8 = share(b0 + (1 - f) * 2 * q + s * q, q, 8, core)
        yield
        c6.wait()
        c9 = share(b0 + (1 - f) * 2 * q + (1 - s) * q, q, 9, core)
        mine = pltpu.make_async_copy(at(full, b0, 4 * q), at(out, b0, 4 * q), osem.at[index, 0])
        mine.start()
        yield
        for cp in (c5, c7, c8, c9):
            cp.wait()
        theirs = off + (1 - c) * 4 * q
        other = pltpu.make_async_copy(at(full, theirs, 4 * q), at(out, theirs, 4 * q), osem.at[index, 1])
        other.start()
        yield
        mine.wait()
        other.wait()

    for cp in loads[:2 * PARTS]:
        cp.wait()
    sketch = dot(right[...], gauss[...], ((0,), (0,)))
    for (kind, i, j), row in where.items():
        if kind == 0:
            buf[row:row + B, :] = sketch[i * B:(i + 1) * B, j * B:(j + 1) * B]
    end = max(starts) + B
    gram_start = streams[counts[0]][0]
    pad = B * sum(k == 0 for k, _, _ in where)
    if pad < gram_start:
        buf[pad:gram_start, :] = jnp.zeros((gram_start - pad, B), F32)
    if end < total:
        buf[end:, :] = jnp.zeros((total - end, B), F32)
    pl.semaphore_wait(barrier, len(partners))

    active = [stream(i) for i in range(counts[0])]
    for g in active:
        next(g)
    for cp in loads[2 * PARTS:]:
        cp.wait()
    step = 2 * B if rank % (2 * B) == 0 else B
    for r in range(0, rank, step):
        g = dot(left[:, r:r + step], left[:, r:], ((0,), (0,)))
        for i in range(r // B, (r + step) // B):
            for j in range(i, rank // B):
                row = where[(1, i, j)]
                buf[row:row + B, :] = g[i * B - r:(i + 1) * B - r, j * B - r:(j + 1) * B - r]
    late = [stream(counts[0] + i) for i in range(counts[1])]
    for g in late:
        next(g)
    active = active + late
    while active:
        active = [g for g in active if next(g, 0) != 0]


def reduced(left, right, gauss):
    modes = lax.axis_size("modes")
    rows, rank = right.shape
    target = gauss.shape[1]
    streams, _, total = plan(rank, target, modes)
    nz = modes // 4
    dma = pltpu.SemaphoreType.DMA
    landing = []
    for _, p, _ in streams:
        q = nz * p
        landing += [pltpu.VMEM((4 * q, B), F32), pltpu.VMEM((2 * q, B), F32), pltpu.VMEM((q, B), F32), pltpu.VMEM((nz - 1, p, B), F32)]
    return pl.pallas_call(
        functools.partial(reduce_kernel, modes),
        out_shape=jax.ShapeDtypeStruct((total, B), F32),
        in_specs=[pl.BlockSpec(memory_space=pl.ANY)] * 3,
        out_specs=pl.BlockSpec(memory_space=pl.ANY),
        scratch_shapes=[
            pltpu.VMEM((rows, rank), BF16),
            pltpu.VMEM((rows, rank), BF16),
            pltpu.VMEM((rows, target), BF16),
            pltpu.VMEM((total, B), F32),
            pltpu.VMEM((total, B), F32),
            *landing,
            dma((3, PARTS)),
            dma((len(streams), 2)),
            dma((len(streams), 10)),
            dma((len(streams), 10)),
            dma((len(streams), 2, nz - 1)),
            dma((len(streams), 2, nz - 1)),
        ],
        compiler_params=pltpu.CompilerParams(collective_id=0, has_side_effects=True, vmem_limit_bytes=61 << 20),
    )(left, right, gauss)


def factor_inverse(block, spl, rowbuf):
    n = B // T
    row = lax.broadcasted_iota(jnp.int32, (T, B), 0)
    lane = lax.broadcasted_iota(jnp.int32, (T, B), 1)
    A = [block[t * T:(t + 1) * T, :] for t in range(n)]
    M = [(row + t * T == lane).astype(F32) for t in range(n)]
    out = []
    for p in range(n):
        k0 = p * T
        for j in range(T):
            spl[p % 2, j] = jnp.broadcast_to(A[p][:, k0 + j:k0 + j + 1], (T, B))
        s = [[jnp.broadcast_to(spl[p % 2, j, i:i + 1, :], (T, B)) if j <= i else None for j in range(T)] for i in range(T)]
        w = [[None] * T for _ in range(T)]
        rs, rd = [], []
        for k in range(T):
            r = lax.rsqrt(s[k][k])
            rs.append(r)
            rd.append(r * r)
            for i in range(k + 1, T):
                w[i][k] = s[i][k] * rd[k]
            for j in range(k + 1, T):
                for i in range(j, T):
                    s[i][j] = s[i][j] - w[i][k] * s[j][k]
        rowbuf[p % 2, 0] = A[p]
        rowbuf[p % 2, 1] = M[p]
        xa = [jnp.broadcast_to(rowbuf[p % 2, 0, i:i + 1, :], (T, B)) for i in range(T)]
        xm = [jnp.broadcast_to(rowbuf[p % 2, 1, i:i + 1, :], (T, B)) for i in range(T)]
        for k in range(T):
            for i in range(k + 1, T):
                xa[i] = xa[i] - w[i][k] * xa[k]
                xm[i] = xm[i] - w[i][k] * xm[k]
        o = xm[0] * rs[0]
        for i in range(1, T):
            o = jnp.where(row == i, xm[i] * rs[i], o)
        out.append(o)
        if p + 1 == n:
            break
        va = [xa[i] * rd[i] for i in range(T)]
        vm = [xm[i] * rd[i] for i in range(T)]
        for k in range(T - 1, 0, -1):
            for i in range(k):
                va[i] = va[i] - w[k][i] * va[k]
                vm[i] = vm[i] - w[k][i] * vm[k]
        for t in range(p + 1, n):
            da = dm = None
            for j in range(T):
                cj = jnp.broadcast_to(A[t][:, k0 + j:k0 + j + 1], (T, B))
                da = cj * va[j] if da is None else da + cj * va[j]
                dm = cj * vm[j] if dm is None else dm + cj * vm[j]
            A[t] = A[t] - da
            M[t] = M[t] - dm
    return jnp.concatenate(out, axis=0)


def halves(v):
    hi = v.astype(BF16)
    return hi, (v - hi.astype(F32)).astype(BF16)


def product(a, b):
    ah, al = halves(a)
    bh, bl = halves(b)
    nn = ((1,), (0,))
    return dot(ah, bh, nn) + (dot(ah, bl, nn) + dot(al, bh, nn))


def solve_kernel(scale, modes, full_hbm, left_hbm, right_hbm, left_new, right_new, full, left, right, lout, rout, sk, gm, spl, rowbuf, fsem, isem, osem):
    high = lax.Precision.HIGHEST
    rows, rank, target = left.shape[0], left.shape[1], lout.shape[1]
    step = rows // PARTS
    parts = [pl.ds(k * step, step) for k in range(PARTS)]
    blocks = list(zip(block_list(rank, target), first_rows(rank, target, modes)))
    chunk = full.shape[0] // FULL_PARTS
    gets = []
    for k in range(FULL_PARTS):
        cp = pltpu.make_async_copy(full_hbm.at[pl.ds(k * chunk, chunk), :], full.at[pl.ds(k * chunk, chunk), :], fsem.at[k])
        cp.start()
        gets.append(cp)
    for cp in gets:
        cp.wait()
    loads = []
    for index, (src, dst) in enumerate(((left_hbm, left), (right_hbm, right))):
        for k, part in enumerate(parts):
            cp = pltpu.make_async_copy(src.at[part, :], dst.at[part, :], isem.at[index, k])
            cp.start()
            loads.append(cp)
    for (kind, i, j), pos in blocks:
        v = full[pos:pos + B, :]
        if kind == 0:
            sk[j * B:(j + 1) * B, i * B:(i + 1) * B] = v.T
        else:
            gm[i * B:(i + 1) * B, j * B:(j + 1) * B] = v
            if i != j:
                gm[j * B:(j + 1) * B, i * B:(i + 1) * B] = v.T
    nn, nt = ((1,), (0,)), ((1,), (1,))
    st = sk[...]
    cross = dot(st, gm[...], nn, high)
    gram = dot(cross, st, nt, high)
    nb = target // B
    low, inv = [], []
    for r in range(nb):
        diag = gram[r * B:(r + 1) * B, r * B:(r + 1) * B]
        if r:
            prev = inv[0] if r == 1 else jnp.concatenate(inv, axis=0)
            lr = dot(gram[r * B:(r + 1) * B, :r * B], prev, nt, high)
            diag = diag - dot(lr, lr, nt, high)
        mi = factor_inverse(diag, spl, rowbuf)
        if r:
            rest = -dot(mi, dot(lr, prev, nn, high), nn, high)
            mi = jnp.concatenate([rest, mi], axis=1)
            inv = [jnp.concatenate([v, jnp.zeros((B, B), F32)], axis=1) for v in inv]
        inv.append(mi)
    inverse = inv[0] if nb == 1 else jnp.concatenate(inv, axis=0)
    wh, wl = halves(product(inverse, st) * scale)
    ph, plo = halves(product(inverse, cross) * (1.0 / scale))
    for cp in loads:
        cp.wait()
    stores = []
    for index, (src, hi, lo, out, dst) in enumerate(((left, wh, wl, lout, left_new), (right, ph, plo, rout, right_new))):
        for k, part in enumerate(parts):
            v = src[part, :]
            out[part, :] = (dot(v, hi, nt) + dot(v, lo, nt)).astype(BF16)
            cp = pltpu.make_async_copy(out.at[part, :], dst.at[part, :], osem.at[index, k])
            cp.start()
            stores.append(cp)
    for cp in stores:
        cp.wait()


def local(left_core, right_core, gauss_core):
    rows, rank = left_core.shape
    target = gauss_core.shape[1]
    devices = lax.axis_size("modes") * lax.axis_size("grp")
    full = reduced(left_core, right_core, gauss_core)
    out = jax.ShapeDtypeStruct((rows, target), BF16)
    return pl.pallas_call(
        functools.partial(solve_kernel, math.sqrt(rows * devices), lax.axis_size("modes")),
        out_shape=(out, out),
        in_specs=[pl.BlockSpec(memory_space=pl.ANY)] * 3,
        out_specs=(pl.BlockSpec(memory_space=pl.ANY),) * 2,
        scratch_shapes=[
            pltpu.VMEM(full.shape, F32),
            pltpu.VMEM((rows, rank), BF16),
            pltpu.VMEM((rows, rank), BF16),
            pltpu.VMEM((rows, target), BF16),
            pltpu.VMEM((rows, target), BF16),
            pltpu.VMEM((target, rank), F32),
            pltpu.VMEM((rank, rank), F32),
            pltpu.VMEM((2, T, T, B), F32),
            pltpu.VMEM((2, 2, T, B), F32),
            pltpu.SemaphoreType.DMA((FULL_PARTS,)),
            pltpu.SemaphoreType.DMA((2, PARTS)),
            pltpu.SemaphoreType.DMA((2, PARTS)),
        ],
        compiler_params=pltpu.CompilerParams(vmem_limit_bytes=61 << 20),
    )(full, left_core, right_core)


def solution(mesh):
    spec = P(("modes", "grp"), None)
    return jax.shard_map(local, mesh=mesh, in_specs=(spec,) * 3, out_specs=(spec, spec), check_vma=False)
```
